256 devices in a mesh: ctx: 64 (over y, z, core), tp: 4 (over x).
Axes of the slice: x: 4, y: 4, z: 8, core: 2. Of those that a mesh axis runs over, the one named last changes fastest.
Arguments:
- queries: bfloat16 [32768, 4096], P(('ctx', 'tp')), may hold values from -6 to 6
- key_states: bfloat16 [32768, 512], P(('ctx', 'tp')), may hold values from -6 to 6
- value_projection: bfloat16 [32768, 512], P(('ctx', 'tp')), may hold values from -6 to 6
- output_gradient: bfloat16 [32768, 4096], P(('ctx', 'tp')), may hold values from -6 to 6
- doc_ids: int32 [32768], replicated, may hold values from 0 to 127, never falling along the last dimension, each value on 1 to 1536 neighbouring positions
- pair_live: int32 [64, 4], P('ctx'), may hold values from 0 to 1, as said below
Outputs:
- attention: bfloat16 [32768, 4096], P('ctx', 'tp')
- query_grad: bfloat16 [32768, 4096], P('ctx', 'tp')
- key_grad: bfloat16 [32768, 512], P('ctx', 'tp')
- value_grad: bfloat16 [32768, 512], P('ctx', 'tp')
The draws below stay inside these ranges and needn't reach their ends.
Inputs may be any that keep to these rules, and one draw needn't show every extreme that they name: `pair_live`: entry [b, 0] is 1; entry [b, r] is 0 where r > b.
All inputs are finite; a program needn't handle non-finite values.
Results may differ from the reference program's by a relative error of at most 0.02.
Values may be sent and summed in bfloat16 or wider, within the bound.
No kernel may reach another device: no remote copies, remote signals or barrier semaphores. Data moves between devices by JAX's collectives and lax.ppermute only.
A program may use at most 64 MiB of HBM per device.

```python
import math
import jax
import jax.numpy as jnp
import numpy as np
from jax import lax

HQ = 32
KEY_VALUE_HEADS = 4
HEAD_SIZE = 128
HEADS_PER_GROUP = 8
TOK_DEV = 512
PAIRS = 4
NBLK = 64
PACKED_TOKENS = 32768
DOCS = 128


def draw_queries(key, part):
    key = jax.random.fold_in(key, 11)
    sampled_values = jnp.clip(jax.random.normal(key, (PACKED_TOKENS, HQ * HEAD_SIZE), jnp.float32), -6.0, 6.0)
    return sampled_values.astype(jnp.bfloat16)


def draw_key_states(key, part):
    key = jax.random.fold_in(key, 12)
    sampled_values = jnp.clip(jax.random.normal(key, (PACKED_TOKENS, KEY_VALUE_HEADS * HEAD_SIZE), jnp.float32), -6.0, 6.0)
    return sampled_values.astype(jnp.bfloat16)


def draw_pair_live(key, part):
    key = jax.random.fold_in(key, 13)
    raw_draw = jax.random.randint(key, (NBLK, PAIRS), 0, 4)
    live_pairs = (raw_draw > 0).astype(jnp.int32)
    offsets = jnp.arange(PAIRS, dtype=jnp.int32)[None, :]
    blocks = jnp.arange(NBLK, dtype=jnp.int32)[:, None]
    live_pairs = jnp.where(offsets == 0, 1, live_pairs)
    live_pairs = jnp.where(offsets > blocks, 0, live_pairs)
    return live_pairs.astype(jnp.int32)


def levels(key, dims, pieces, low, top_value):
    loudness = 1.0
    for position, shards_of in pieces:
        heights = jax.random.uniform(jax.random.fold_in(jax.random.fold_in(key, 6), position), (shards_of,), jnp.float32, low / len(pieces), top_value / len(pieces))
        loudness = loudness * jnp.repeat(jnp.exp(heights), dims[position] // shards_of).reshape((-1,) + (1,) * (len(dims) - 1 - position))
    return loudness


def profile(amount, total, limit, slope):
    portions = [(1 << 20) // math.isqrt(standing ** slope) + 1 for standing in range(2, amount + 1)]
    spare, given = total - limit - (amount - 1), [1] * (amount - 1)
    while spare > 0:
        free = [i for i in range(amount - 1) if given[i] < limit]
        mass, left = sum([portions[i] for i in free]), spare
        for i in free:
            extra = min(limit - given[i], max(1, left * portions[i] // mass), spare)
            given[i] = given[i] + extra
            spare = spare - extra
    return np.array([limit] + given)


def ragged_sizes(rng, number_of, total, most, skew):
    if number_of == 2:
        one = jax.random.randint(rng, (), max(1, total - most), min(most, total - 1) + 1)
        return jnp.stack([one, total - one])
    sizes = jnp.asarray(profile(number_of, total, most, skew), jnp.int32)
    twos = (number_of - 1) // 2
    donor, sink = sizes[1:1 + 2 * twos:2], sizes[2:2 + 2 * twos:2]
    slack = jnp.minimum(donor - 1, most - sink)
    moved = jax.random.randint(jax.random.fold_in(rng, 1), (twos,), 0, 1 << 20) % (slack + 1)
    sizes = sizes.at[1:1 + 2 * twos:2].set(donor - moved).at[2:2 + 2 * twos:2].set(sink + moved)
    return sizes[jax.random.permutation(jax.random.fold_in(rng, 2), number_of)]


def centred(stream_key, extent, scale, most, pieces=(), held_as=jnp.bfloat16):
    gain = levels(stream_key, extent, pieces, -0.22, 0.18) if pieces else 1.0
    array = jax.random.normal(stream_key, extent, jnp.float32) * scale * gain
    return jnp.minimum(jnp.maximum(array, -most), most).astype(held_as)


def setup_inputs(seed: int = 0) -> dict:
    arg_keys = jax.random.split(jax.random.key(seed), 7)
    queries = draw_queries(jax.random.fold_in(arg_keys[6], 71), 0)
    key_states = draw_key_states(jax.random.fold_in(arg_keys[6], 71), 0)
    value_projection = centred(arg_keys[2], (PACKED_TOKENS, KEY_VALUE_HEADS * HEAD_SIZE), 1.0, 6.0, ((0, 256),))
    output_gradient = centred(arg_keys[3], (PACKED_TOKENS, HQ * HEAD_SIZE), 1.0, 6.0, ((0, 256),))
    doc_ids = jnp.searchsorted(jnp.cumsum(ragged_sizes(arg_keys[4], DOCS, PACKED_TOKENS, (PAIRS - 1) * TOK_DEV, 2)), jnp.arange(PACKED_TOKENS), side="right").astype(jnp.int32)
    pair_live = draw_pair_live(jax.random.fold_in(arg_keys[6], 71), 0)
    return dict(queries=queries, key_states=key_states, value_projection=value_projection, output_gradient=output_gradient, doc_ids=doc_ids, pair_live=pair_live)


def build_mask(doc_ids, pair_row, blk_index, rows_per_block):
    positions = jnp.arange(rows_per_block, dtype=jnp.int32)
    query_start = (blk_index * rows_per_block).astype(jnp.int32)
    query_ids = lax.dynamic_slice_in_dim(doc_ids, query_start, rows_per_block)
    mask_list = []
    for offset in range(PAIRS):
        key_block = (blk_index - offset).astype(jnp.int32)
        key_start = (jnp.maximum(key_block, 0) * rows_per_block).astype(jnp.int32)
        key_ids = lax.dynamic_slice_in_dim(doc_ids, key_start, rows_per_block)
        same_doc = query_ids[:, None] == key_ids[None, :]
        causal = (key_block * rows_per_block + positions)[None, :] <= (query_start + positions)[:, None]
        live_pair = (pair_row[offset] == 1) & (key_block >= 0)
        mask_list.append(same_doc & causal & live_pair)
    return jnp.concatenate(mask_list, axis=1)


def reference(queries, key_states, value_projection, output_gradient, doc_ids, pair_live):
    rows_per_block = TOK_DEV
    scaling = HEAD_SIZE ** -0.5
    key_value_width = KEY_VALUE_HEADS * HEAD_SIZE
    joined = jnp.concatenate([key_states, value_projection], axis=1)

    def one_block(running, blk_index):
        start_offset = (blk_index * rows_per_block).astype(jnp.int32)
        query_tile_block = lax.dynamic_slice_in_dim(queries, start_offset, rows_per_block).astype(jnp.float32).reshape(rows_per_block, KEY_VALUE_HEADS, HEADS_PER_GROUP, HEAD_SIZE)
        gradient_block = lax.dynamic_slice_in_dim(output_gradient, start_offset, rows_per_block).astype(jnp.float32).reshape(rows_per_block, KEY_VALUE_HEADS, HEADS_PER_GROUP, HEAD_SIZE)
        collected_rows = []
        for offset in range(PAIRS):
            key_start = (jnp.maximum(blk_index - offset, 0) * rows_per_block).astype(jnp.int32)
            collected_rows.append(lax.dynamic_slice_in_dim(joined, key_start, rows_per_block))
        collected_rows = jnp.concatenate(collected_rows, axis=0).astype(jnp.float32)
        key_tile_block = collected_rows[:, :key_value_width].reshape(-1, KEY_VALUE_HEADS, HEAD_SIZE)
        value_tile_block = collected_rows[:, key_value_width:].reshape(-1, KEY_VALUE_HEADS, HEAD_SIZE)
        allowed = build_mask(doc_ids, pair_live[blk_index], blk_index, rows_per_block)
        scores = jnp.einsum("qghd,kgd->ghqk", query_tile_block, key_tile_block) * scaling
        scores = jnp.where(allowed[None, None], scores, -1e30)
        row_max = jnp.max(scores, axis=3, keepdims=True)
        exponent = jnp.exp(scores - row_max)
        attn_probs = exponent / jnp.sum(exponent, axis=3, keepdims=True)
        probs_low = lax.optimization_barrier(attn_probs.astype(jnp.bfloat16)).astype(jnp.float32)
        output = jnp.einsum("ghqk,kgd->qghd", probs_low, value_tile_block).astype(jnp.bfloat16)
        prob_grad = jnp.einsum("qghd,kgd->ghqk", gradient_block, value_tile_block)
        row_delta = jnp.sum(gradient_block * output.astype(jnp.float32), axis=3)
        row_delta = jnp.transpose(row_delta, (1, 2, 0))[..., None]
        score_grad = lax.optimization_barrier((attn_probs * (prob_grad - row_delta)).astype(jnp.bfloat16)).astype(jnp.float32)
        query_grad = (jnp.einsum("ghqk,kgd->qghd", score_grad, key_tile_block) * scaling).astype(jnp.bfloat16)
        key_part = jnp.einsum("ghqk,qghd->kgd", score_grad, query_tile_block) * scaling
        value_part = jnp.einsum("ghqk,qghd->kgd", probs_low, gradient_block)
        gradients = jnp.concatenate([key_part.reshape(-1, key_value_width), value_part.reshape(-1, key_value_width)], axis=1)
        gradients = gradients.reshape(PAIRS, rows_per_block, 2 * key_value_width)
        for offset in range(PAIRS):
            target = (jnp.maximum(blk_index - offset, 0) * rows_per_block).astype(jnp.int32)
            current = lax.dynamic_slice_in_dim(running, target, rows_per_block)
            running = lax.dynamic_update_slice_in_dim(running, current + gradients[offset], target, 0)
        return running, (output.reshape(rows_per_block, -1), query_grad.reshape(rows_per_block, -1))

    zero_grad = jnp.zeros((PACKED_TOKENS, 2 * key_value_width), jnp.float32)
    summed, (out_list, grad_list) = lax.scan(one_block, zero_grad, jnp.arange(NBLK, dtype=jnp.int32))
    attention = out_list.reshape(PACKED_TOKENS, HQ * HEAD_SIZE)
    query_grad = grad_list.reshape(PACKED_TOKENS, HQ * HEAD_SIZE)
    return attention, query_grad, summed[:, :key_value_width].astype(jnp.bfloat16), summed[:, key_value_width:].astype(jnp.bfloat16)
```

```python
import functools
import math

import jax
import jax.numpy as jnp
from jax import lax
from jax.experimental import pallas as pl
from jax.experimental.pallas import tpu as pltpu
from jax.sharding import PartitionSpec as P

HEAD_SIZE = 128
HEADS_PER_GROUP = 8
PAIRS = 4
BLOCK = 512
TQ = 128
TILES = BLOCK // TQ
LANES = HEADS_PER_GROUP * TQ
TK = 256
CHUNK = 256
SCALING = HEAD_SIZE ** (-0.5)
LOG2_SCALING = SCALING * math.log2(math.e)
MASKED = -2e30
LOWEST = -1e30
F32 = jnp.float32
BF16 = jnp.bfloat16


def dot_nt(a, b):
    return lax.dot_general(a, b, (((1,), (1,)), ((), ())), preferred_element_type=F32)


def dot_nn(a, b):
    return lax.dot_general(a, b, (((1,), (0,)), ((), ())), preferred_element_type=F32)


def tile_bias(lo_row, tile, key_start):
    keys = lax.broadcasted_iota(jnp.int32, (TK, TQ), 0) + key_start
    last = lax.broadcasted_iota(jnp.int32, (TK, TQ), 1) + ((PAIRS - 1) * BLOCK + tile * TQ)
    bias = jnp.where((keys >= lo_row) & (keys <= last), 0.0, MASKED).astype(F32)
    return jnp.concatenate([bias] * (CHUNK // TQ), axis=1)


def step_range(scalars, tile, offset):
    base = (PAIRS - 1 - offset) * BLOCK
    first = jnp.maximum(scalars[tile] - base, 0) // TK
    per_block = BLOCK // TK
    last = (tile * TQ) // TK + 1 if offset == 0 else per_block
    first = jnp.where(scalars[TILES + offset] == 1, first, per_block)
    return first, last


def forward_kernel(scalars, q_ref, kv0, kv1, kv2, kv3, lo_ref, out_ref, lse_ref, m_s, l_s, acc_s, vt_s):
    tile = pl.program_id(0)
    kvs = (kv0, kv1, kv2, kv3)

    @pl.when(tile == 0)
    def _():
        for offset in range(PAIRS):
            for part in range(BLOCK // TQ):
                vt_s[offset, :, part * TQ : (part + 1) * TQ] = kvs[offset][part, 1].T

    m_s[...] = jnp.full_like(m_s, LOWEST)
    l_s[...] = jnp.zeros_like(l_s)
    acc_s[...] = jnp.zeros_like(acc_s)
    lo_row = lo_ref[0]
    for offset in range(PAIRS - 1, -1, -1):
        kv = kvs[offset]
        base = (PAIRS - 1 - offset) * BLOCK

        def step(i, carry, kv=kv, base=base, offset=offset):
            key = kv[pl.ds(i * (TK // TQ), TK // TQ), 0].reshape(TK, HEAD_SIZE)
            val_t = vt_s[offset, :, pl.ds(pl.multiple_of(i * TK, TK), TK)]
            bias = tile_bias(lo_row, tile, base + i * TK)
            for c in range(LANES // CHUNK):
                lanes = slice(c * CHUNK, (c + 1) * CHUNK)
                s = dot_nt(key, q_ref[0, lanes, :]) * LOG2_SCALING + bias
                m_old = m_s[:, lanes]
                m_new = jnp.maximum(m_old, jnp.max(s, axis=0, keepdims=True))
                alpha = jnp.exp2(m_old - m_new)
                p = jnp.exp2(s - m_new)
                l_s[:, lanes] = l_s[:, lanes] * alpha + jnp.sum(p, axis=0, keepdims=True)
                m_s[:, lanes] = m_new
                acc_s[:, lanes] = acc_s[:, lanes] * alpha + dot_nn(val_t, p.astype(BF16))
            return carry

        first, last = step_range(scalars, tile, offset)
        lax.fori_loop(first, last, step, 0)
    total = l_s[...]
    lse_ref[0] = m_s[...] + jnp.log2(total)
    result = acc_s[...] * (1.0 / total)
    for h in range(HEADS_PER_GROUP):
        cols = slice(h * TQ, (h + 1) * TQ)
        out_ref[:, cols] = result[:, cols].T.astype(BF16)


def delta_kernel(out_ref, do_ref, delta_ref):
    ones = jnp.ones((8, HEAD_SIZE), BF16)
    for h in range(HEADS_PER_GROUP):
        cols = slice(h * TQ, (h + 1) * TQ)
        product = out_ref[:, cols].astype(F32) * do_ref[0, cols, :].astype(F32)
        high = product.astype(BF16)
        low = (product - high.astype(F32)).astype(BF16)
        delta_ref[0, :, cols] = (dot_nt(ones, high) + dot_nt(ones, low))[0:1]


def backward_kernel(offsets, first_call, last_call, scalars, *refs):
    n = len(offsets)
    q_ref, do_ref = refs[:2]
    kvs = refs[2 : 2 + n]
    lo_ref, lse_ref, delta_ref = refs[2 + n : 5 + n]
    refs = refs[5 + n :]
    if not first_call:
        dq_in, refs = refs[0], refs[1:]
    dq_ref = refs[0]
    outs = refs[1 : 1 + n]
    dkv_s, dqt_s, kt_s = refs[1 + n :]
    tile = pl.program_id(0)

    @pl.when(tile == 0)
    def _():
        dkv_s[...] = jnp.zeros_like(dkv_s)
        for slot in range(n):
            for part in range(BLOCK // TQ):
                kt_s[slot, :, part * TQ : (part + 1) * TQ] = kvs[slot][part, 0].T

    if first_call:
        dqt_s[...] = jnp.zeros_like(dqt_s)
    else:
        dqt_s[...] = dq_in[0]
    lo_row = lo_ref[0]
    for slot, offset in enumerate(offsets):
        kv = kvs[slot]
        base = (PAIRS - 1 - offset) * BLOCK

        def step(i, carry, kv=kv, base=base, slot=slot):
            key = kv[pl.ds(i * (TK // TQ), TK // TQ), 0].reshape(TK, HEAD_SIZE)
            val = kv[pl.ds(i * (TK // TQ), TK // TQ), 1].reshape(TK, HEAD_SIZE)
            rows = pl.ds(pl.multiple_of(i * TK, TK), TK)
            key_t = kt_s[slot, :, rows]
            bias = tile_bias(lo_row, tile, base + i * TK)
            dk = dkv_s[slot, 0, rows, :]
            dv = dkv_s[slot, 1, rows, :]
            for c in range(LANES // CHUNK):
                lanes = slice(c * CHUNK, (c + 1) * CHUNK)
                q = q_ref[0, lanes, :]
                do = do_ref[0, lanes, :]
                s = dot_nt(key, q) * LOG2_SCALING + bias
                p = jnp.exp2(s - lse_ref[0, :, lanes])
                dp = dot_nt(val, do)
                ds = (p * (dp - delta_ref[0, :, lanes])).astype(BF16)
                dv = dv + dot_nn(p.astype(BF16), do)
                dk = dk + dot_nn(ds, q)
                dqt_s[:, lanes] += dot_nn(key_t, ds)
            dkv_s[slot, 0, rows, :] = dk
            dkv_s[slot, 1, rows, :] = dv
            return carry

        first, last = step_range(scalars, tile, offset)
        lax.fori_loop(first, last, step, 0)

    if last_call:
        for h in range(HEADS_PER_GROUP):
            cols = slice(h * TQ, (h + 1) * TQ)
            dq_ref[:, cols] = (dqt_s[:, cols] * SCALING).T.astype(BF16)
    else:
        dq_ref[0] = dqt_s[...]

    @pl.when(tile == TILES - 1)
    def _():
        for slot, offset in enumerate(offsets):
            kind = outs[slot].dtype
            for part in range(BLOCK // TQ):
                rows = slice(part * TQ, (part + 1) * TQ)
                outs[slot][part, 0] = (dkv_s[slot, 0, rows, :] * SCALING).astype(kind)
                outs[slot][part, 1] = dkv_s[slot, 1, rows, :].astype(kind)


def spec_smem():
    return pl.BlockSpec(memory_space=pltpu.SMEM)


def spec_tile(rows, cols):
    return pl.BlockSpec((1, rows, cols), lambda t: (t, 0, 0))


def spec_kv():
    return pl.BlockSpec((TILES, 2, TQ, HEAD_SIZE), lambda t: (0, 0, 0, 0))


def params():
    return pltpu.CompilerParams(
        dimension_semantics=("arbitrary",), vmem_limit_bytes=40 * 1024 * 1024
    )


def forward(scalars, q, kvs, lo):
    return pl.pallas_call(
        forward_kernel,
        grid=(TILES,),
        in_specs=[spec_smem(), spec_tile(LANES, HEAD_SIZE)]
        + [spec_kv()] * PAIRS
        + [spec_tile(1, TQ)],
        out_specs=[pl.BlockSpec((TQ, LANES), lambda t: (t, 0)), spec_tile(1, LANES)],
        out_shape=[
            jax.ShapeDtypeStruct((BLOCK, LANES), BF16),
            jax.ShapeDtypeStruct((TILES, 1, LANES), F32),
        ],
        scratch_shapes=[
            pltpu.VMEM((1, LANES), F32),
            pltpu.VMEM((1, LANES), F32),
            pltpu.VMEM((HEAD_SIZE, LANES), F32),
            pltpu.VMEM((PAIRS, HEAD_SIZE, BLOCK), BF16),
        ],
        compiler_params=params(),
        cost_estimate=pl.CostEstimate(
            flops=2 * 2 * 8 * 512 * 1280 * 128 * 2, bytes_accessed=4 << 20, transcendentals=0
        ),
        name="forward",
    )(scalars, q, *kvs, lo)


def deltas(attention, do):
    return pl.pallas_call(
        delta_kernel,
        grid=(TILES,),
        in_specs=[pl.BlockSpec((TQ, LANES), lambda t: (t, 0)), spec_tile(LANES, HEAD_SIZE)],
        out_specs=spec_tile(1, LANES),
        out_shape=jax.ShapeDtypeStruct((TILES, 1, LANES), F32),
        compiler_params=params(),
        name="deltas",
    )(attention, do)


def backward(offsets, scalars, q, do, kvs, lo, lse, delta, dq):
    n = len(offsets)
    first_call, last_call = dq is None, 0 in offsets
    dq_spec = spec_tile(HEAD_SIZE, LANES)
    dq_shape = jax.ShapeDtypeStruct((TILES, HEAD_SIZE, LANES), F32)
    out_spec, out_shape = dq_spec, dq_shape
    if last_call:
        out_spec = pl.BlockSpec((TQ, LANES), lambda t: (t, 0))
        out_shape = jax.ShapeDtypeStruct((BLOCK, LANES), BF16)
    return pl.pallas_call(
        functools.partial(backward_kernel, offsets, first_call, last_call),
        grid=(TILES,),
        in_specs=[spec_smem(), spec_tile(LANES, HEAD_SIZE), spec_tile(LANES, HEAD_SIZE)]
        + [spec_kv()] * n
        + [spec_tile(1, TQ), spec_tile(1, LANES), spec_tile(1, LANES)]
        + ([] if first_call else [dq_spec]),
        out_specs=[out_spec] + [spec_kv()] * n,
        out_shape=[out_shape]
        + [
            jax.ShapeDtypeStruct((TILES, 2, TQ, HEAD_SIZE), F32 if offset == 0 else BF16)
            for offset in offsets
        ],
        scratch_shapes=[
            pltpu.VMEM((n, 2, BLOCK, HEAD_SIZE), F32),
            pltpu.VMEM((HEAD_SIZE, LANES), F32),
            pltpu.VMEM((n, HEAD_SIZE, BLOCK), BF16),
        ],
        compiler_params=params(),
        cost_estimate=pl.CostEstimate(
            flops=2 * 5 * 8 * 512 * 512 * n * 128 * 2, bytes_accessed=4 << 20, transcendentals=0
        ),
        name="backward_" + "_".join(map(str, offsets)),
    )(scalars, q, do, *kvs, lo, lse, delta, *([] if first_call else [dq]))


def passed_along(value, axis, steps):
    count = lax.axis_size(axis)
    initial, last = (max(0, -steps), min(count, count - steps))
    return lax.ppermute(value, axis, [(source, source + steps) for source in range(initial, last)])


def by_head(value):
    tokens = value.shape[0]
    return jnp.transpose(value.reshape(tokens, -1, HEAD_SIZE), (1, 0, 2))


def exchange(value):
    return lax.all_to_all(value, "tp", split_axis=0, concat_axis=0, tiled=True)


def window_start(doc_ids, blk):
    begin = jnp.maximum(blk - (PAIRS - 1), 0) * BLOCK
    window = lax.dynamic_slice_in_dim(doc_ids, begin, PAIRS * BLOCK)
    own = lax.dynamic_slice_in_dim(doc_ids, blk * BLOCK, BLOCK)
    before = jnp.sum((window[:, None] < own[None, :]).astype(jnp.int32), axis=0)
    return before + begin - (blk - (PAIRS - 1)) * BLOCK


def bounds(lo, live):
    return lo.reshape(TILES, 1, TQ), jnp.concatenate([lo[::TQ], live])


def local(queries, key_states, value_projection, output_gradient, doc_ids, pair_live):
    blk = lax.axis_index("ctx")
    kv = jnp.stack([by_head(key_states), by_head(value_projection)], axis=1)
    kv = exchange(kv)
    q = exchange(by_head(queries)).reshape(TILES, LANES, HEAD_SIZE)
    kvs = [kv] + [passed_along(kv, "ctx", offset) for offset in range(1, PAIRS)]
    do = exchange(by_head(output_gradient)).reshape(TILES, LANES, HEAD_SIZE)
    lo, scalars = bounds(window_start(doc_ids, blk), pair_live[0])
    attention, lse = forward(scalars, q, kvs, lo)
    delta = deltas(attention, do)
    dq, part3, part2 = backward((3, 2), scalars, q, do, [kvs[3], kvs[2]], lo, lse, delta, None)
    got3 = passed_along(part3, "ctx", -3)
    got2 = passed_along(part2, "ctx", -2)
    dq, part1 = backward((1,), scalars, q, do, [kvs[1]], lo, lse, delta, dq)
    got1 = passed_along(part1, "ctx", -1)
    dq, part0 = backward((0,), scalars, q, do, [kvs[0]], lo, lse, delta, dq)
    total = part0 + got1.astype(F32) + got2.astype(F32) + got3.astype(F32)
    key_grad = total[:, 0].reshape(BLOCK, HEAD_SIZE).astype(BF16)
    value_grad = total[:, 1].reshape(BLOCK, HEAD_SIZE).astype(BF16)
    return (attention, dq, key_grad, value_grad)


def solution(mesh):
    in_specs = (
        P(("ctx", "tp"), None),
        P(("ctx", "tp"), None),
        P(("ctx", "tp"), None),
        P(("ctx", "tp"), None),
        P(),
        P("ctx", None),
    )
    out_specs = (P("ctx", "tp"), P("ctx", "tp"), P("ctx", "tp"), P("ctx", "tp"))
    return jax.shard_map(local, mesh=mesh, in_specs=in_specs, out_specs=out_specs, check_vma=False)
```

```python
import functools
import math

import jax
import jax.numpy as jnp
from jax import lax
from jax.experimental import pallas as pl
from jax.experimental.pallas import tpu as pltpu
from jax.sharding import PartitionSpec as P

HEAD_SIZE = 128
HEADS_PER_GROUP = 8
PAIRS = 4
BLOCK = 512
TQ = 128
TILES = BLOCK // TQ
LANES = HEADS_PER_GROUP * TQ
TK = 256
STEPS = BLOCK // TK
MOST_STEPS = TILES * PAIRS * STEPS + 2
SCALING = HEAD_SIZE ** (-0.5)
LOG2_SCALING = SCALING * math.log2(math.e)
MASKED = -2e30
LOWEST = -1e30
F32 = jnp.float32
BF16 = jnp.bfloat16


def dot_nt(a, b):
    return lax.dot_general(a, b, (((1,), (1,)), ((), ())), preferred_element_type=F32)


def dot_nn(a, b):
    return lax.dot_general(a, b, (((1,), (0,)), ((), ())), preferred_element_type=F32)


def tile_bias(lo_row, tile, key_start):
    keys = lax.broadcasted_iota(jnp.int32, (TK, TQ), 0) + key_start
    last = lax.broadcasted_iota(jnp.int32, (TK, TQ), 1) + ((PAIRS - 1) * BLOCK + tile * TQ)
    return jnp.where((keys >= lo_row) & (keys <= last), 0.0, MASKED).astype(F32)


def list_steps(scalars, offsets, meta):
    count = jnp.int32(0)
    for slot, offset in enumerate(offsets):
        base = (PAIRS - 1 - offset) * BLOCK
        for tile in range(TILES):
            last = (tile * TQ) // TK + 1 if offset == 0 else STEPS
            first = jnp.minimum(jnp.maximum(scalars[tile] - base, 0) // TK, last)
            first = jnp.where(scalars[TILES + offset] == 1, first, last)

            def write(i, n, slot=slot, tile=tile, base=base):
                meta[0, n] = tile
                meta[1, n] = slot * STEPS + i
                meta[2, n] = base + i * TK
                return n + 1

            count = lax.fori_loop(first, last, write, count)
    for extra in range(2):
        meta[0, count + extra] = 0
        meta[1, count + extra] = 0
        meta[2, count + extra] = PAIRS * BLOCK
    return count


def run_steps(count, stage1, stage2, bufs_a, bufs_b):
    stage1(0, bufs_a)

    def body(j, carry):
        stage1(2 * j + 1, bufs_b)
        stage2(2 * j, bufs_a)
        stage1(2 * j + 2, bufs_a)
        stage2(2 * j + 1, bufs_b)
        return carry

    lax.fori_loop(0, (count + 1) // 2, body, 0)


def rows_of(k):
    return pl.ds(pl.multiple_of(k * TK, TK), TK)


def heads_of(ref, tile):
    return ref[tile, 0:HEADS_PER_GROUP].reshape(LANES, HEAD_SIZE)


def pack_kernel(n, *refs):
    refs, out_ref = refs[:-1], refs[-1]
    slot = 0
    for ref in refs:
        for h in range(ref.shape[1] // HEAD_SIZE):
            out_ref[0, slot] = ref[:, h * HEAD_SIZE : (h + 1) * HEAD_SIZE]
            slot += 1


def forward_kernel(scalars, x_ref, kv1, kv2, kv3, lo_ref, out_ref, lse_ref, *scratch):
    m_s, l_s, acc_s, k_s, vt_s, sa_s, sb_s, pa_s, pb_s, meta = scratch
    offsets = (3, 2, 1, 0)
    for slot, kv in enumerate((kv3, kv2, kv1, x_ref)):
        for part in range(TILES):
            place = slice(slot * BLOCK + part * TQ, slot * BLOCK + (part + 1) * TQ)
            k_s[place, :] = kv[part, kv.shape[1] - 2]
            vt_s[:, place] = kv[part, kv.shape[1] - 1].T
    m_s[...] = jnp.full_like(m_s, LOWEST)
    l_s[...] = jnp.zeros_like(l_s)
    acc_s[...] = jnp.zeros_like(acc_s)
    count = list_steps(scalars, offsets, meta)

    def stage1(n, bufs):
        bufs[0][...] = dot_nt(k_s[rows_of(meta[1, n]), :], heads_of(x_ref, meta[0, n]))

    def stage2(n, bufs):
        tile = meta[0, n]
        bias = tile_bias(lo_ref[tile], tile, meta[2, n])
        val_t = vt_s[:, rows_of(meta[1, n])]
        for h in range(HEADS_PER_GROUP):
            lanes = slice(h * TQ, (h + 1) * TQ)
            s = bufs[0][:, lanes] * LOG2_SCALING + bias
            m_old = m_s[tile, :, lanes]
            m_new = jnp.maximum(m_old, jnp.max(s, axis=0, keepdims=True))
            alpha = jnp.exp2(m_old - m_new)
            p = jnp.exp2(s - m_new)
            l_s[tile, :, lanes] = l_s[tile, :, lanes] * alpha + jnp.sum(p, axis=0, keepdims=True)
            m_s[tile, :, lanes] = m_new
            acc_s[tile, :, lanes] = acc_s[tile, :, lanes] * alpha
            bufs[1][:, lanes] = p.astype(BF16)
        acc_s[tile] = acc_s[tile] + dot_nn(val_t, bufs[1][...])

    run_steps(count, stage1, stage2, (sa_s, pa_s), (sb_s, pb_s))
    for tile in range(TILES):
        total = l_s[tile]
        lse_ref[tile] = m_s[tile] + jnp.log2(total)
        inverse = 1.0 / total
        for h in range(HEADS_PER_GROUP):
            cols = slice(h * TQ, (h + 1) * TQ)
            out_ref[tile * TQ : (tile + 1) * TQ, cols] = (
                (acc_s[tile, :, cols] * inverse[:, cols]).T.astype(BF16)
            )


def write_delta(out_ref, do_ref, delta_ref):
    ones = jnp.ones((8, HEAD_SIZE), BF16)
    for tile in range(TILES):
        for h in range(HEADS_PER_GROUP):
            cols = slice(h * TQ, (h + 1) * TQ)
            out = out_ref[tile * TQ : (tile + 1) * TQ, cols]
            product = out.astype(F32) * do_ref[tile, h].astype(F32)
            high = product.astype(BF16)
            low = (product - high.astype(F32)).astype(BF16)
            delta_ref[tile, :, cols] = (dot_nt(ones, high) + dot_nt(ones, low))[0:1]


def backward_kernel(offsets, first_call, last_call, scalars, *refs):
    n = len(offsets)
    x_ref, do_ref = refs[:2]
    remote = len([offset for offset in offsets if offset])
    kvs = refs[2 : 2 + remote] + ((x_ref,) if last_call else ())
    lo_ref, lse_ref = refs[2 + remote : 4 + remote]
    refs = refs[4 + remote :]
    if first_call:
        out_ref, delta_ref, dq_ref = refs[:3]
        write_delta(out_ref, do_ref, delta_ref)
        refs = refs[2:]
    else:
        delta_ref, dq_in, dq_ref = refs[:3]
        refs = refs[2:]
    outs = refs[1 : 1 + n]
    dk_s, dv_s, dqt_s, k_s, v_s, kt_s, sa, sb, da, db, pa, pb, ga, gb, meta = refs[1 + n :]
    if not last_call:
        dqt_s = dq_ref
    for slot, kv in enumerate(kvs):
        for part in range(TILES):
            place = slice(slot * BLOCK + part * TQ, slot * BLOCK + (part + 1) * TQ)
            key = kv[part, kv.shape[1] - 2]
            k_s[place, :] = key
            kt_s[:, place] = key.T
            v_s[place, :] = kv[part, kv.shape[1] - 1]
    dk_s[...] = jnp.zeros_like(dk_s)
    dv_s[...] = jnp.zeros_like(dv_s)
    dqt_s[...] = jnp.zeros_like(dqt_s) if first_call else dq_in[...]
    count = list_steps(scalars, offsets, meta)

    def stage1(i, bufs):
        tile, rows = meta[0, i], rows_of(meta[1, i])
        bufs[0][...] = dot_nt(k_s[rows, :], heads_of(x_ref, tile))
        bufs[1][...] = dot_nt(v_s[rows, :], heads_of(do_ref, tile))

    def stage2(i, bufs):
        s_s, d_s, p_s, g_s = bufs
        tile, rows = meta[0, i], rows_of(meta[1, i])
        bias = tile_bias(lo_ref[tile], tile, meta[2, i])
        for h in range(HEADS_PER_GROUP):
            lanes = slice(h * TQ, (h + 1) * TQ)
            p = jnp.exp2(s_s[:, lanes] * LOG2_SCALING + bias - lse_ref[tile, :, lanes])
            p_s[:, lanes] = p.astype(BF16)
            g_s[:, lanes] = (p * (d_s[:, lanes] - delta_ref[tile, :, lanes])).astype(BF16)
        dv_s[rows, :] += dot_nn(p_s[...], heads_of(do_ref, tile))
        dk_s[rows, :] += dot_nn(g_s[...], heads_of(x_ref, tile))
        dqt_s[tile] += dot_nn(kt_s[:, rows], g_s[...])

    run_steps(count, stage1, stage2, (sa, da, pa, ga), (sb, db, pb, gb))
    if last_call:
        for tile in range(TILES):
            for h in range(HEADS_PER_GROUP):
                cols = slice(h * TQ, (h + 1) * TQ)
                dq_ref[tile * TQ : (tile + 1) * TQ, cols] = (
                    (dqt_s[tile, :, cols] * SCALING).T.astype(BF16)
                )
    for slot, offset in enumerate(offsets):
        kind = outs[slot].dtype
        for part in range(TILES):
            place = slice(slot * BLOCK + part * TQ, slot * BLOCK + (part + 1) * TQ)
            outs[slot][part, 0] = (dk_s[place, :] * SCALING).astype(kind)
            outs[slot][part, 1] = dv_s[place, :].astype(kind)


def vmem():
    return pl.BlockSpec(memory_space=pltpu.VMEM)


def smem():
    return pl.BlockSpec(memory_space=pltpu.SMEM)


def params():
    return pltpu.CompilerParams(vmem_limit_bytes=40 * 1024 * 1024)


def pack(*arrays):
    heads = [array.shape[1] // HEAD_SIZE // TILES for array in arrays]
    tokens = arrays[0].shape[0]
    return pl.pallas_call(
        functools.partial(pack_kernel, len(arrays)),
        grid=(TILES,),
        in_specs=[pl.BlockSpec((tokens, n * HEAD_SIZE), lambda g: (0, g)) for n in heads],
        out_specs=pl.BlockSpec((1, sum(heads), tokens, HEAD_SIZE), lambda g: (g, 0, 0, 0)),
        out_shape=jax.ShapeDtypeStruct((TILES, sum(heads), tokens, HEAD_SIZE), BF16),
        compiler_params=params(),
        name="pack_%d" % len(arrays),
    )(*arrays)


def forward(scalars, x, kvs, lo):
    return pl.pallas_call(
        forward_kernel,
        in_specs=[smem()] + [vmem()] * (PAIRS + 1),
        out_specs=[vmem()] * 2,
        out_shape=[
            jax.ShapeDtypeStruct((BLOCK, LANES), BF16),
            jax.ShapeDtypeStruct((TILES, 1, LANES), F32),
        ],
        scratch_shapes=[
            pltpu.VMEM((TILES, 1, LANES), F32),
            pltpu.VMEM((TILES, 1, LANES), F32),
            pltpu.VMEM((TILES, HEAD_SIZE, LANES), F32),
            pltpu.VMEM((PAIRS * BLOCK, HEAD_SIZE), BF16),
            pltpu.VMEM((HEAD_SIZE, PAIRS * BLOCK), BF16),
            pltpu.VMEM((TK, LANES), F32),
            pltpu.VMEM((TK, LANES), F32),
            pltpu.VMEM((TK, LANES), BF16),
            pltpu.VMEM((TK, LANES), BF16),
            pltpu.SMEM((3, MOST_STEPS), jnp.int32),
        ],
        compiler_params=params(),
        cost_estimate=pl.CostEstimate(
            flops=2 * 2 * 8 * 512 * 1280 * 128 * 2, bytes_accessed=4 << 20, transcendentals=0
        ),
        name="forward",
    )(scalars, x, *kvs, lo)


def backward(offsets, scalars, x, do, kvs, lo, lse, extra):
    n = len(offsets)
    first_call, last_call = len(extra) == 1, 0 in offsets
    out_shape = [jax.ShapeDtypeStruct((TILES, HEAD_SIZE, LANES), F32)]
    if last_call:
        out_shape = [jax.ShapeDtypeStruct((BLOCK, LANES), BF16)]
    if first_call:
        out_shape = [jax.ShapeDtypeStruct((TILES, 1, LANES), F32)] + out_shape
    return pl.pallas_call(
        functools.partial(backward_kernel, offsets, first_call, last_call),
        in_specs=[smem()] + [vmem()] * (4 + len(kvs) + len(extra)),
        out_specs=[vmem()] * (len(out_shape) + n),
        out_shape=out_shape
        + [
            jax.ShapeDtypeStruct((TILES, 2, TQ, HEAD_SIZE), F32 if offset == 0 else BF16)
            for offset in offsets
        ],
        scratch_shapes=[
            pltpu.VMEM((n * BLOCK, HEAD_SIZE), F32),
            pltpu.VMEM((n * BLOCK, HEAD_SIZE), F32),
            pltpu.VMEM((TILES if last_call else 1, HEAD_SIZE, LANES), F32),
            pltpu.VMEM((n * BLOCK, HEAD_SIZE), BF16),
            pltpu.VMEM((n * BLOCK, HEAD_SIZE), BF16),
            pltpu.VMEM((HEAD_SIZE, n * BLOCK), BF16),
        ]
        + [pltpu.VMEM((TK, LANES), F32)] * 4
        + [pltpu.VMEM((TK, LANES), BF16)] * 4
        + [pltpu.SMEM((3, MOST_STEPS), jnp.int32)],
        compiler_params=params(),
        cost_estimate=pl.CostEstimate(
            flops=2 * 5 * 8 * 512 * 512 * n * 128 * 2, bytes_accessed=4 << 20, transcendentals=0
        ),
        name="backward_" + "_".join(map(str, offsets)),
    )(scalars, x, do, *kvs, lo, lse, *extra)


def passed_along(value, axis, steps):
    count = lax.axis_size(axis)
    initial, last = (max(0, -steps), min(count, count - steps))
    return lax.ppermute(value, axis, [(source, source + steps) for source in range(initial, last)])


def exchange(value):
    return lax.all_to_all(value, "tp", split_axis=0, concat_axis=0, tiled=True)


def window_start(doc_ids, blk):
    begin = jnp.maximum(blk - (PAIRS - 1), 0) * BLOCK
    window = lax.dynamic_slice_in_dim(doc_ids, begin, PAIRS * BLOCK)
    own = lax.dynamic_slice_in_dim(doc_ids, blk * BLOCK, BLOCK)
    before = jnp.sum((window[:, None] < own[None, :]).astype(jnp.int32), axis=0)
    return before + begin - (blk - (PAIRS - 1)) * BLOCK


def bounds(lo, live):
    return lo.reshape(TILES, 1, TQ), jnp.concatenate([lo[::TQ], live])


def local(queries, key_states, value_projection, output_gradient, doc_ids, pair_live):
    blk = lax.axis_index("ctx")
    x = exchange(pack(queries, key_states, value_projection))
    lo, scalars = bounds(window_start(doc_ids, blk), pair_live[0])
    kv = x[:, HEADS_PER_GROUP:]
    kvs = [passed_along(kv, "ctx", offset) for offset in range(1, PAIRS)]
    do = exchange(pack(output_gradient))
    attention, lse = forward(scalars, x, kvs, lo)
    kv1, kv2, kv3 = kvs
    delta, dq, part3, part2 = backward((3, 2), scalars, x, do, [kv3, kv2], lo, lse, [attention])
    got3 = passed_along(part3, "ctx", -3)
    got2 = passed_along(part2, "ctx", -2)
    dq, part1 = backward((1,), scalars, x, do, [kv1], lo, lse, [delta, dq])
    got1 = passed_along(part1, "ctx", -1)
    dq, part0 = backward((0,), scalars, x, do, [], lo, lse, [delta, dq])
    total = part0 + got1.astype(F32) + got2.astype(F32) + got3.astype(F32)
    key_grad = total[:, 0].reshape(BLOCK, HEAD_SIZE).astype(BF16)
    value_grad = total[:, 1].reshape(BLOCK, HEAD_SIZE).astype(BF16)
    return (attention, dq, key_grad, value_grad)


def solution(mesh):
    in_specs = (
        P(("ctx", "tp"), None),
        P(("ctx", "tp"), None),
        P(("ctx", "tp"), None),
        P(("ctx", "tp"), None),
        P(),
        P("ctx", None),
    )
    out_specs = (P("ctx", "tp"), P("ctx", "tp"), P("ctx", "tp"), P("ctx", "tp"))
    return jax.shard_map(local, mesh=mesh, in_specs=in_specs, out_specs=out_specs, check_vma=False)
```

```python
import functools
import math

import jax
import jax.numpy as jnp
from jax import lax
from jax.experimental import pallas as pl
from jax.experimental.pallas import tpu as pltpu
from jax.sharding import PartitionSpec as P

HEAD_SIZE = 128
HEADS_PER_GROUP = 8
PAIRS = 4
BLOCK = 512
TQ = 128
TILES = BLOCK // TQ
LANES = HEADS_PER_GROUP * TQ
TK = 256
STEPS = BLOCK // TK
MOST_STEPS = TILES * PAIRS * STEPS
OFFSETS = (3, 2, 1, 0)
SUMS = HEAD_SIZE + 8
SCALING = HEAD_SIZE ** (-0.5)
LOG2_SCALING = SCALING * math.log2(math.e)
MASKED = -2e30
LOWEST = -1e30
F32 = jnp.float32
BF16 = jnp.bfloat16


def dot_nt(a, b):
    return lax.dot_general(a, b, (((1,), (1,)), ((), ())), preferred_element_type=F32)


def dot_nn(a, b):
    return lax.dot_general(a, b, (((1,), (0,)), ((), ())), preferred_element_type=F32)


def tile_bias(lo_row, tile, key_start):
    keys = lax.broadcasted_iota(jnp.int32, (TK, TQ), 0) + key_start
    last = lax.broadcasted_iota(jnp.int32, (TK, TQ), 1) + ((PAIRS - 1) * BLOCK + tile * TQ)
    return jnp.where((keys >= lo_row) & (keys <= last), 0.0, MASKED).astype(F32)


def list_steps(scalars, meta):
    count = jnp.int32(0)
    for slot, offset in enumerate(OFFSETS):
        base = (PAIRS - 1 - offset) * BLOCK
        for tile in range(TILES):
            last = (tile * TQ) // TK + 1 if offset == 0 else STEPS
            first = jnp.minimum(jnp.maximum(scalars[tile] - base, 0) // TK, last)
            first = jnp.where(scalars[TILES + offset] == 1, first, last)

            def write(i, n, slot=slot, tile=tile, base=base):
                meta[0, n] = tile
                meta[1, n] = slot * STEPS + i
                meta[2, n] = base + i * TK
                return n + 1

            count = lax.fori_loop(first, last, write, count)
    for extra in range(2):
        meta[0, count + extra] = 0
        meta[1, count + extra] = 0
        meta[2, count + extra] = PAIRS * BLOCK
    return count


def run_steps(count, stage1, stage2, buf_a, buf_b):
    stage1(0, buf_a)

    def body(j, carry):
        stage1(2 * j + 1, buf_b)
        stage2(2 * j, buf_a)
        stage1(2 * j + 2, buf_a)
        stage2(2 * j + 1, buf_b)
        return carry

    lax.fori_loop(0, (count + 1) // 2, body, 0)


def rows_of(k):
    return pl.ds(pl.multiple_of(k * TK, TK), TK)


def pack_kernel(*refs):
    refs, out_ref = refs[:-1], refs[-1]
    groups = out_ref.shape[0]
    slot = 0
    for ref in refs:
        per_group = ref.shape[1] // HEAD_SIZE // groups
        for group in range(groups):
            for h in range(per_group):
                head = group * per_group + h
                out_ref[group, slot + h] = ref[:, head * HEAD_SIZE : (head + 1) * HEAD_SIZE]
        slot += per_group


def attend_kernel(heads, first_head, first_call, last_call, scalars, x_ref, *refs):
    kvs, lo_ref, refs = refs[0:PAIRS], refs[PAIRS], refs[PAIRS + 1 :]
    if not first_call:
        dk_in, dv_in, refs = refs[0], refs[1], refs[4:]
    att_ref, dq_ref, refs = refs[0], refs[1], refs[2:]
    if last_call:
        outs, refs = refs[0:PAIRS], refs[PAIRS:]
    else:
        dk_out, dv_out, refs = refs[0], refs[1], refs[2:]
    m_s, acc_s, dqt_s, dk_s, dv_s, delta_s, k_s, kt_s, v_s, vt_s = refs[:10]
    buf_a, buf_b, stash_s, top_s, att_s, meta, sem = refs[10:]
    lanes_all = heads * TQ
    if not last_call:
        dk_s, dv_s = dk_out, dv_out

    def queries(tile):
        return x_ref[tile, 0:heads].reshape(lanes_all, HEAD_SIZE)

    def cotangents(tile):
        return x_ref[tile, heads : 2 * heads].reshape(lanes_all, HEAD_SIZE)

    def columns(h):
        return slice(h * TQ, (h + 1) * TQ)

    def put(tile, ref, kind):
        return pltpu.make_async_copy(
            att_s.at[tile],
            ref.at[pl.ds(tile * TQ, TQ), pl.ds(first_head * TQ, lanes_all)],
            sem.at[kind, tile],
        )

    for slot, kv in enumerate(reversed(kvs)):
        for part in range(TILES):
            place = slice(slot * BLOCK + part * TQ, slot * BLOCK + (part + 1) * TQ)
            key, value = kv[part, 0], kv[part, 1]
            k_s[place, :] = key
            kt_s[:, place] = key.T
            v_s[place, :] = value
            vt_s[0:HEAD_SIZE, place] = value.T
    vt_s[HEAD_SIZE:SUMS, :] = jnp.ones((SUMS - HEAD_SIZE, PAIRS * BLOCK), BF16)
    m_s[...] = jnp.full_like(m_s, LOWEST)
    acc_s[...] = jnp.zeros_like(acc_s)
    count = list_steps(scalars, meta)

    def scores(n, buf):
        buf[...] = dot_nt(k_s[rows_of(meta[1, n]), :], queries(meta[0, n]))

    def weigh(n, buf):
        tile = meta[0, n]
        bias = tile_bias(lo_ref[tile], tile, meta[2, n])
        val_t = vt_s[:, rows_of(meta[1, n])]
        m_old = m_s[tile]
        weights, tops = [], []
        for h in range(heads):
            s = buf[:, columns(h)] * LOG2_SCALING + bias
            top = jnp.maximum(m_old[:, columns(h)], jnp.max(s, axis=0, keepdims=True))
            weights.append(jnp.exp2(s - top).astype(BF16))
            tops.append(top)
        p = jnp.concatenate(weights, axis=1)
        m_new = jnp.concatenate(tops, axis=1)
        stash_s[n] = p
        top_s[n] = m_new
        m_s[tile] = m_new
        acc_s[tile] = acc_s[tile] * jnp.exp2(m_old - m_new) + dot_nn(val_t, p)

    run_steps(count, scores, weigh, buf_a, buf_b)
    ones = jnp.ones((8, HEAD_SIZE), BF16)
    for tile in range(TILES):
        total = acc_s[tile, HEAD_SIZE : HEAD_SIZE + 1, :]
        m_s[tile] = m_s[tile] + jnp.log2(total)
        inverse = 1.0 / total
        for h in range(heads):
            out = (acc_s[tile, 0:HEAD_SIZE, columns(h)] * inverse[:, columns(h)]).astype(BF16).T
            att_s[tile, :, columns(h)] = out
            product = out.astype(F32) * x_ref[tile, heads + h].astype(F32)
            high = product.astype(BF16)
            low = (product - high.astype(F32)).astype(BF16)
            delta_s[tile, :, columns(h)] = (dot_nt(ones, high) + dot_nt(ones, low))[0:1]
        put(tile, att_ref, 0).start()
    if first_call:
        dk_s[...] = jnp.zeros_like(dk_s)
        dv_s[...] = jnp.zeros_like(dv_s)
    else:
        dk_s[...] = dk_in[...]
        dv_s[...] = dv_in[...]
    dqt_s[...] = jnp.zeros_like(dqt_s)

    def prob_grads(n, buf):
        buf[...] = dot_nt(v_s[rows_of(meta[1, n]), :], cotangents(meta[0, n]))

    def gradients(n, buf):
        tile, rows = meta[0, n], rows_of(meta[1, n])
        factor = jnp.exp2(top_s[n] - m_s[tile])
        delta = delta_s[tile]
        weights, grads = [], []
        for h in range(heads):
            p = stash_s[n, :, columns(h)].astype(F32) * factor[:, columns(h)]
            weights.append(p.astype(BF16))
            grads.append((p * (buf[:, columns(h)] - delta[:, columns(h)])).astype(BF16))
        p = jnp.concatenate(weights, axis=1)
        g = jnp.concatenate(grads, axis=1)
        dv_s[rows, :] += dot_nn(p, cotangents(tile))
        dk_s[rows, :] += dot_nn(g, queries(tile))
        dqt_s[tile] += dot_nn(kt_s[:, rows], g)

    run_steps(count, prob_grads, gradients, buf_a, buf_b)
    for tile in range(TILES):
        put(tile, att_ref, 0).wait()
        for h in range(heads):
            att_s[tile, :, columns(h)] = (dqt_s[tile, :, columns(h)] * SCALING).astype(BF16).T
        put(tile, dq_ref, 1).start()
    if last_call:
        for slot in range(PAIRS):
            kind = outs[slot].dtype
            for part in range(TILES):
                place = slice(slot * BLOCK + part * TQ, slot * BLOCK + (part + 1) * TQ)
                outs[slot][part, 0] = (dk_s[place, :] * SCALING).astype(kind)
                outs[slot][part, 1] = dv_s[place, :].astype(kind)
    for tile in range(TILES):
        put(tile, dq_ref, 1).wait()


def vmem():
    return pl.BlockSpec(memory_space=pltpu.VMEM)


def smem():
    return pl.BlockSpec(memory_space=pltpu.SMEM)


def pack(*arrays, steps=1, limit=40):
    heads = sum(array.shape[1] // HEAD_SIZE // TILES for array in arrays)
    tokens = arrays[0].shape[0]
    return pl.pallas_call(
        pack_kernel,
        grid=(steps,),
        in_specs=[
            pl.BlockSpec((tokens, array.shape[1] // steps), lambda g: (0, g)) for array in arrays
        ],
        out_specs=pl.BlockSpec(
            (TILES // steps, heads, tokens, HEAD_SIZE), lambda g: (g, 0, 0, 0)
        ),
        out_shape=jax.ShapeDtypeStruct((TILES, heads, tokens, HEAD_SIZE), BF16),
        compiler_params=pltpu.CompilerParams(vmem_limit_bytes=limit << 20),
        name="pack_%d" % len(arrays),
    )(*arrays)


def attend(scalars, x, kvs, lo, first_head, carried):
    rows = PAIRS * BLOCK
    heads = x.shape[1] // 2
    lanes = heads * TQ
    first_call, last_call = not carried, first_head + heads == HEADS_PER_GROUP
    hbm = pl.BlockSpec(memory_space=pltpu.HBM)
    result = jax.ShapeDtypeStruct((BLOCK, LANES), BF16)
    sums = [jax.ShapeDtypeStruct((rows, HEAD_SIZE), F32)] * 2
    grad_shape = (TILES, 2, TQ, HEAD_SIZE)
    parts = [jax.ShapeDtypeStruct(grad_shape, F32 if o == 0 else BF16) for o in OFFSETS]
    more = parts if last_call else sums
    return pl.pallas_call(
        functools.partial(attend_kernel, heads, first_head, first_call, last_call),
        in_specs=[smem()] + [vmem()] * (PAIRS + 2) + [vmem(), vmem(), hbm, hbm][: len(carried)],
        out_specs=[hbm, hbm] + [vmem()] * len(more),
        out_shape=[result, result] + more,
        input_output_aliases={} if first_call else {PAIRS + 5: 0, PAIRS + 6: 1},
        scratch_shapes=[
            pltpu.VMEM((TILES, 1, lanes), F32),
            pltpu.VMEM((TILES, SUMS, lanes), F32),
            pltpu.VMEM((TILES, HEAD_SIZE, lanes), F32),
            pltpu.VMEM((rows if last_call else 8, HEAD_SIZE), F32),
            pltpu.VMEM((rows if last_call else 8, HEAD_SIZE), F32),
            pltpu.VMEM((TILES, 1, lanes), F32),
            pltpu.VMEM((rows, HEAD_SIZE), BF16),
            pltpu.VMEM((HEAD_SIZE, rows), BF16),
            pltpu.VMEM((rows, HEAD_SIZE), BF16),
            pltpu.VMEM((SUMS, rows), BF16),
            pltpu.VMEM((TK, lanes), F32),
            pltpu.VMEM((TK, lanes), F32),
            pltpu.VMEM((MOST_STEPS, TK, lanes), BF16),
            pltpu.VMEM((MOST_STEPS, 1, lanes), F32),
            pltpu.VMEM((TILES, TQ, lanes), BF16),
            pltpu.SMEM((3, MOST_STEPS), jnp.int32),
            pltpu.SemaphoreType.DMA((2, TILES)),
        ],
        compiler_params=pltpu.CompilerParams(vmem_limit_bytes=(12 + 3 * heads) << 20),
        cost_estimate=pl.CostEstimate(
            flops=2 * 6 * heads * 512 * 1280 * 128 * 2, bytes_accessed=8 << 20, transcendentals=0
        ),
        name="attend_%d" % first_head,
    )(scalars, x, *kvs, lo, *carried)


def passed_along(value, axis, steps):
    count = lax.axis_size(axis)
    initial, last = (max(0, -steps), min(count, count - steps))
    return lax.ppermute(value, axis, [(source, source + steps) for source in range(initial, last)])


def exchange(value):
    return lax.all_to_all(value, "tp", split_axis=0, concat_axis=0, tiled=True)


def window_start(doc_ids, blk):
    begin = jnp.maximum(blk - (PAIRS - 1), 0) * BLOCK
    window = lax.dynamic_slice_in_dim(doc_ids, begin, PAIRS * BLOCK)
    own = lax.dynamic_slice_in_dim(doc_ids, blk * BLOCK, BLOCK)
    before = jnp.sum((window[:, None] < own[None, :]).astype(jnp.int32), axis=0)
    return before + begin - (blk - (PAIRS - 1)) * BLOCK


def bounds(lo, live):
    return lo.reshape(TILES, 1, TQ), jnp.concatenate([lo[::TQ], live])


def local(queries, key_states, value_projection, output_gradient, doc_ids, pair_live):
    blk = lax.axis_index("ctx")
    kv0 = exchange(pack(key_states, value_projection, limit=60))
    x = exchange(pack(queries, output_gradient, steps=4, limit=60))
    lo, scalars = bounds(window_start(doc_ids, blk), pair_live[0])
    kv2 = passed_along(kv0, "ctx", 2)
    kv1 = passed_along(kv0, "ctx", 1)
    kv3 = passed_along(kv2, "ctx", 1)
    kvs = [kv0, kv1, kv2, kv3]
    attention, dq, part3, part2, part1, part0 = attend(scalars, x, kvs, lo, 0, ())
    got3 = passed_along(part3, "ctx", -1)
    got1 = passed_along(part1, "ctx", -1)
    part2 = (part2.astype(F32) + got3.astype(F32)).astype(BF16)
    got2 = passed_along(part2, "ctx", -2)
    total = part0 + got1.astype(F32) + got2.astype(F32)
    key_grad = total[:, 0].reshape(BLOCK, HEAD_SIZE).astype(BF16)
    value_grad = total[:, 1].reshape(BLOCK, HEAD_SIZE).astype(BF16)
    return (attention, dq, key_grad, value_grad)


def solution(mesh):
    in_specs = (
        P(("ctx", "tp"), None),
        P(("ctx", "tp"), None),
        P(("ctx", "tp"), None),
        P(("ctx", "tp"), None),
        P(),
        P("ctx", None),
    )
    out_specs = (P("ctx", "tp"), P("ctx", "tp"), P("ctx", "tp"), P("ctx", "tp"))
    return jax.shard_map(local, mesh=mesh, in_specs=in_specs, out_specs=out_specs, check_vma=False)
```

```python
import functools
import math

import jax
import jax.numpy as jnp
from jax import lax
from jax.experimental import pallas as pl
from jax.experimental.pallas import tpu as pltpu
from jax.sharding import PartitionSpec as P

HEAD_SIZE = 128
HEADS_PER_GROUP = 8
PAIRS = 4
BLOCK = 512
TQ = 128
TILES = BLOCK // TQ
LANES = HEADS_PER_GROUP * TQ
TK = 256
MOST_STEPS = 32
OFFSETS = (3, 2, 1, 0)
SUMS = HEAD_SIZE + 8
SCALING = HEAD_SIZE ** (-0.5)
LOG2_SCALING = SCALING * math.log2(math.e)
MASKED = -2e30
LOWEST = -1e30
F32 = jnp.float32
BF16 = jnp.bfloat16


def dot_nt(a, b):
    return lax.dot_general(a, b, (((1,), (1,)), ((), ())), preferred_element_type=F32)


def dot_nn(a, b):
    return lax.dot_general(a, b, (((1,), (0,)), ((), ())), preferred_element_type=F32)


def step_bias(lo_row, meta, n):
    start, first, last = meta[1, n], meta[2, n], meta[3, n]
    own = lax.broadcasted_iota(jnp.int32, (1, TQ), 1) + ((PAIRS - 1) * BLOCK + meta[0, n] * TQ)
    keys = lax.broadcasted_iota(jnp.int32, (TK, TQ), 0) + start
    seen = (keys >= jnp.maximum(lo_row, first)) & (keys <= jnp.minimum(own, last))
    return jnp.where(seen, 0.0, MASKED).astype(F32)


def list_steps(scalars, meta):
    count = jnp.int32(0)
    for tile in range(TILES):
        end = (PAIRS - 1) * BLOCK + (tile + 1) * TQ
        while end > 0:
            start = max(end - TK, 0)
            block = start // BLOCK
            border = (block + 1) * BLOCK
            first = jnp.where(scalars[TILES + PAIRS - 1 - block] == 1, start, border)
            last = jnp.int32(end - 1)
            if border < end:
                last = jnp.where(scalars[TILES + PAIRS - 2 - block] == 1, last, border - 1)
            meta[0, count] = tile
            meta[1, count] = start
            meta[2, count] = first
            meta[3, count] = last
            used = jnp.maximum(first, scalars[tile]) <= last
            count = count + used.astype(jnp.int32)
            end = end - TK
    for extra in range(2):
        meta[0, count + extra] = 0
        meta[1, count + extra] = 0
        meta[2, count + extra] = PAIRS * BLOCK
        meta[3, count + extra] = 0
    return count


def run_steps(count, stage1, stage2, buf_a, buf_b):
    stage1(0, buf_a)

    def body(j, carry):
        stage1(2 * j + 1, buf_b)
        stage2(2 * j, buf_a)
        stage1(2 * j + 2, buf_a)
        stage2(2 * j + 1, buf_b)
        return carry

    lax.fori_loop(0, (count + 1) // 2, body, 0)


def rows_of(start):
    return pl.ds(pl.multiple_of(start, TQ), TK)


def pack_kernel(q_ref, do_ref, x_ref, wide_s, x_s, in_sem, out_sem):
    width = HEADS_PER_GROUP * HEAD_SIZE
    wide = [
        [
            pltpu.make_async_copy(
                ref.at[:, pl.ds(group * width, width)], wide_s.at[i, group], in_sem.at[i, group]
            )
            for i, ref in enumerate((q_ref, do_ref))
        ]
        for group in range(TILES)
    ]
    for copy in sum(wide, []):
        copy.start()
    out_copies = []
    for group in range(TILES):
        for i in range(2):
            wide[group][i].wait()
            for h in range(HEADS_PER_GROUP):
                piece = wide_s[i, group, :, h * HEAD_SIZE : (h + 1) * HEAD_SIZE]
                x_s[group, i * HEADS_PER_GROUP + h] = piece
        out_copies.append(pltpu.make_async_copy(x_s.at[group], x_ref.at[group], out_sem.at[group]))
        out_copies[-1].start()
    for copy in out_copies:
        copy.wait()


def pack_kv_kernel(place, key_ref, value_ref, *outs):
    for d, out_ref in enumerate(outs):
        group = (place[0] + d) % TILES
        columns = pl.ds(pl.multiple_of(group * HEAD_SIZE, HEAD_SIZE), HEAD_SIZE)
        out_ref[0] = key_ref[:, columns]
        out_ref[1] = value_ref[:, columns]


def attend_kernel(heads, first_head, first_call, last_call, scalars, x_ref, *refs):
    kvs, lo_ref, refs = refs[0:PAIRS], refs[PAIRS], refs[PAIRS + 1 :]
    if not first_call:
        dk_in, dv_in, refs = refs[0], refs[1], refs[4:]
    att_ref, dq_ref, refs = refs[0], refs[1], refs[2:]
    if last_call:
        outs, refs = refs[0:PAIRS], refs[PAIRS:]
    else:
        dk_out, dv_out, refs = refs[0], refs[1], refs[2:]
    m_s, acc_s, dqt_s, dk_s, dv_s, delta_s, k_s, kt_s, v_s, vt_s = refs[:10]
    buf_a, buf_b, stash_s, top_s, att_s, meta, sem = refs[10:]
    lanes_all = heads * TQ
    if not last_call:
        dk_s, dv_s = dk_out, dv_out

    def queries(tile):
        return x_ref[tile, 0:heads].reshape(lanes_all, HEAD_SIZE)

    def cotangents(tile):
        return x_ref[tile, heads : 2 * heads].reshape(lanes_all, HEAD_SIZE)

    def columns(h):
        return slice(h * TQ, (h + 1) * TQ)

    def put(tile, ref, kind):
        return pltpu.make_async_copy(
            att_s.at[tile],
            ref.at[pl.ds(tile * TQ, TQ), pl.ds(first_head * TQ, lanes_all)],
            sem.at[kind, tile],
        )

    for slot, kv in enumerate(reversed(kvs)):
        for part in range(TILES):
            tokens = (scalars[2 * TILES] + TILES - part) % TILES
            place = pl.ds(pl.multiple_of(slot * BLOCK + tokens * TQ, TQ), TQ)
            key, value = kv[part, 0], kv[part, 1]
            k_s[place, :] = key
            kt_s[:, place] = key.T
            v_s[place, :] = value
            vt_s[0:HEAD_SIZE, place] = value.T
    vt_s[HEAD_SIZE:SUMS, :] = jnp.ones((SUMS - HEAD_SIZE, PAIRS * BLOCK), BF16)
    m_s[...] = jnp.full_like(m_s, LOWEST)
    acc_s[...] = jnp.zeros_like(acc_s)
    count = list_steps(scalars, meta)

    def scores(n, buf):
        buf[...] = dot_nt(k_s[rows_of(meta[1, n]), :], queries(meta[0, n]))

    def weigh(n, buf):
        tile = meta[0, n]
        bias = step_bias(lo_ref[tile], meta, n)
        val_t = vt_s[:, rows_of(meta[1, n])]
        m_old = m_s[tile]
        weights, tops = [], []
        for h in range(heads):
            s = buf[:, columns(h)] * LOG2_SCALING + bias
            top = jnp.maximum(m_old[:, columns(h)], jnp.max(s, axis=0, keepdims=True))
            weights.append(jnp.exp2(s - top).astype(BF16))
            tops.append(top)
        p = jnp.concatenate(weights, axis=1)
        m_new = jnp.concatenate(tops, axis=1)
        stash_s[n] = p
        top_s[n] = m_new
        m_s[tile] = m_new
        acc_s[tile] = acc_s[tile] * jnp.exp2(m_old - m_new) + dot_nn(val_t, p)

    run_steps(count, scores, weigh, buf_a, buf_b)
    ones = jnp.ones((8, HEAD_SIZE), BF16)
    for tile in range(TILES):
        total = acc_s[tile, HEAD_SIZE : HEAD_SIZE + 1, :]
        m_s[tile] = m_s[tile] + jnp.log2(total)
        inverse = 1.0 / total
        for h in range(heads):
            out = (acc_s[tile, 0:HEAD_SIZE, columns(h)] * inverse[:, columns(h)]).astype(BF16).T
            att_s[tile, :, columns(h)] = out
            product = out.astype(F32) * x_ref[tile, heads + h].astype(F32)
            high = product.astype(BF16)
            low = (product - high.astype(F32)).astype(BF16)
            delta_s[tile, :, columns(h)] = (dot_nt(ones, high) + dot_nt(ones, low))[0:1]
        put(tile, att_ref, 0).start()
    if first_call:
        dk_s[...] = jnp.zeros_like(dk_s)
        dv_s[...] = jnp.zeros_like(dv_s)
    else:
        dk_s[...] = dk_in[...]
        dv_s[...] = dv_in[...]
    dqt_s[...] = jnp.zeros_like(dqt_s)

    def prob_grads(n, buf):
        buf[...] = dot_nt(v_s[rows_of(meta[1, n]), :], cotangents(meta[0, n]))

    def gradients(n, buf):
        tile, rows = meta[0, n], rows_of(meta[1, n])
        factor = jnp.exp2(top_s[n] - m_s[tile])
        delta = delta_s[tile]
        weights, grads = [], []
        for h in range(heads):
            p = stash_s[n, :, columns(h)].astype(F32) * factor[:, columns(h)]
            weights.append(p.astype(BF16))
            grads.append((p * (buf[:, columns(h)] - delta[:, columns(h)])).astype(BF16))
        p = jnp.concatenate(weights, axis=1)
        g = jnp.concatenate(grads, axis=1)
        dv_s[rows, :] += dot_nn(p, cotangents(tile))
        dk_s[rows, :] += dot_nn(g, queries(tile))
        dqt_s[tile] += dot_nn(kt_s[:, rows], g)

    run_steps(count, prob_grads, gradients, buf_a, buf_b)
    for tile in range(TILES):
        put(tile, att_ref, 0).wait()
        for h in range(heads):
            att_s[tile, :, columns(h)] = (dqt_s[tile, :, columns(h)] * SCALING).astype(BF16).T
        put(tile, dq_ref, 1).start()
    if last_call:
        for slot in range(PAIRS):
            kind = outs[slot].dtype
            for part in range(TILES):
                place = slice(slot * BLOCK + part * TQ, slot * BLOCK + (part + 1) * TQ)
                outs[slot][part, 0] = (dk_s[place, :] * SCALING).astype(kind)
                outs[slot][part, 1] = dv_s[place, :].astype(kind)
    for tile in range(TILES):
        put(tile, dq_ref, 1).wait()


def vmem():
    return pl.BlockSpec(memory_space=pltpu.VMEM)


def smem():
    return pl.BlockSpec(memory_space=pltpu.SMEM)


def pack(queries, cotangents):
    tokens = queries.shape[0]
    hbm = pl.BlockSpec(memory_space=pltpu.HBM)
    both = (TILES, 2 * HEADS_PER_GROUP, tokens, HEAD_SIZE)
    return pl.pallas_call(
        pack_kernel,
        in_specs=[hbm] * 2,
        out_specs=hbm,
        out_shape=jax.ShapeDtypeStruct(both, BF16),
        scratch_shapes=[
            pltpu.VMEM((2, TILES, tokens, HEADS_PER_GROUP * HEAD_SIZE), BF16),
            pltpu.VMEM(both, BF16),
            pltpu.SemaphoreType.DMA((2, TILES)),
            pltpu.SemaphoreType.DMA((TILES,)),
        ],
        compiler_params=pltpu.CompilerParams(vmem_limit_bytes=60 << 20),
        name="pack",
    )(queries, cotangents)


def pack_kv(place, keys, values):
    shape = jax.ShapeDtypeStruct((2, keys.shape[0], HEAD_SIZE), BF16)
    return pl.pallas_call(
        pack_kv_kernel,
        in_specs=[smem(), vmem(), vmem()],
        out_specs=[vmem()] * TILES,
        out_shape=[shape] * TILES,
        name="pack_kv",
    )(place, keys, values)


def attend(scalars, x, kvs, lo, first_head, carried):
    rows = PAIRS * BLOCK
    heads = x.shape[1] // 2
    lanes = heads * TQ
    first_call, last_call = not carried, first_head + heads == HEADS_PER_GROUP
    hbm = pl.BlockSpec(memory_space=pltpu.HBM)
    result = jax.ShapeDtypeStruct((BLOCK, LANES), BF16)
    sums = [jax.ShapeDtypeStruct((rows, HEAD_SIZE), F32)] * 2
    grad_shape = (TILES, 2, TQ, HEAD_SIZE)
    parts = [jax.ShapeDtypeStruct(grad_shape, F32 if o == 0 else BF16) for o in OFFSETS]
    more = parts if last_call else sums
    return pl.pallas_call(
        functools.partial(attend_kernel, heads, first_head, first_call, last_call),
        in_specs=[smem()] + [vmem()] * (PAIRS + 2) + [vmem(), vmem(), hbm, hbm][: len(carried)],
        out_specs=[hbm, hbm] + [vmem()] * len(more),
        out_shape=[result, result] + more,
        input_output_aliases={} if first_call else {PAIRS + 5: 0, PAIRS + 6: 1},
        scratch_shapes=[
            pltpu.VMEM((TILES, 1, lanes), F32),
            pltpu.VMEM((TILES, SUMS, lanes), F32),
            pltpu.VMEM((TILES, HEAD_SIZE, lanes), F32),
            pltpu.VMEM((rows if last_call else 8, HEAD_SIZE), F32),
            pltpu.VMEM((rows if last_call else 8, HEAD_SIZE), F32),
            pltpu.VMEM((TILES, 1, lanes), F32),
            pltpu.VMEM((rows, HEAD_SIZE), BF16),
            pltpu.VMEM((HEAD_SIZE, rows), BF16),
            pltpu.VMEM((rows, HEAD_SIZE), BF16),
            pltpu.VMEM((SUMS, rows), BF16),
            pltpu.VMEM((TK, lanes), F32),
            pltpu.VMEM((TK, lanes), F32),
            pltpu.VMEM((MOST_STEPS, TK, lanes), BF16),
            pltpu.VMEM((MOST_STEPS, 1, lanes), F32),
            pltpu.VMEM((TILES, TQ, lanes), BF16),
            pltpu.SMEM((4, MOST_STEPS), jnp.int32),
            pltpu.SemaphoreType.DMA((2, TILES)),
        ],
        compiler_params=pltpu.CompilerParams(vmem_limit_bytes=(12 + 3 * heads) << 20),
        cost_estimate=pl.CostEstimate(
            flops=2 * 6 * heads * 512 * 1280 * 128 * 2, bytes_accessed=8 << 20, transcendentals=0
        ),
        name="attend_%d" % first_head,
    )(scalars, x, *kvs, lo, *carried)


def passed_along(value, axis, steps):
    count = lax.axis_size(axis)
    initial, last = (max(0, -steps), min(count, count - steps))
    return lax.ppermute(value, axis, [(source, source + steps) for source in range(initial, last)])


def exchange(value):
    return lax.all_to_all(value, "tp", split_axis=0, concat_axis=0, tiled=True)


def window_start(doc_ids, blk):
    begin = jnp.maximum(blk - (PAIRS - 1), 0) * BLOCK
    window = lax.dynamic_slice_in_dim(doc_ids, begin, PAIRS * BLOCK)
    own = lax.dynamic_slice_in_dim(doc_ids, blk * BLOCK, BLOCK)
    before = jnp.sum((window[:, None] < own[None, :]).astype(jnp.int32), axis=0)
    return before + begin - (blk - (PAIRS - 1)) * BLOCK


def bounds(lo, live, place):
    return lo.reshape(TILES, 1, TQ), jnp.concatenate([lo[::TQ], live, place])


def local(queries, key_states, value_projection, output_gradient, doc_ids, pair_live):
    blk = lax.axis_index("ctx")
    place = lax.axis_index("tp").astype(jnp.int32).reshape(1)
    own, *pieces = pack_kv(place, key_states, value_projection)
    for d, piece in enumerate(pieces, start=1):
        pieces[d - 1] = lax.ppermute(piece, "tp", [(i, (i + d) % TILES) for i in range(TILES)])
    queries, output_gradient, own = lax.optimization_barrier((queries, output_gradient, own))
    x = pack(queries, output_gradient)
    x, own, *pieces = lax.optimization_barrier((x, own, *pieces))
    x = exchange(x)
    kv0 = jnp.stack([own] + pieces)
    lo, scalars = bounds(window_start(doc_ids, blk), pair_live[0], place)
    kv2 = passed_along(kv0, "ctx", 2)
    kv1 = passed_along(kv0, "ctx", 1)
    kv3 = passed_along(kv2, "ctx", 1)
    kvs = [kv0, kv1, kv2, kv3]
    attention, dq, part3, part2, part1, part0 = attend(scalars, x, kvs, lo, 0, ())
    got3 = passed_along(part3, "ctx", -1)
    got1 = passed_along(part1, "ctx", -1)
    part2 = (part2.astype(F32) + got3.astype(F32)).astype(BF16)
    got2 = passed_along(part2, "ctx", -2)
    total = part0 + got1.astype(F32) + got2.astype(F32)
    key_grad = total[:, 0].reshape(BLOCK, HEAD_SIZE).astype(BF16)
    value_grad = total[:, 1].reshape(BLOCK, HEAD_SIZE).astype(BF16)
    return (attention, dq, key_grad, value_grad)


def solution(mesh):
    in_specs = (
        P(("ctx", "tp"), None),
        P(("ctx", "tp"), None),
        P(("ctx", "tp"), None),
        P(("ctx", "tp"), None),
        P(),
        P("ctx", None),
    )
    out_specs = (P("ctx", "tp"), P("ctx", "tp"), P("ctx", "tp"), P("ctx", "tp"))
    return jax.shard_map(local, mesh=mesh, in_specs=in_specs, out_specs=out_specs, check_vma=False)
```

```python
import functools
import math

import jax
import jax.numpy as jnp
from jax import lax
from jax.experimental import pallas as pl
from jax.experimental.pallas import tpu as pltpu
from jax.sharding import PartitionSpec as P

HEAD_SIZE = 128
HEADS_PER_GROUP = 8
PAIRS = 4
BLOCK = 512
TQ = 128
TILES = BLOCK // TQ
LANES = HEADS_PER_GROUP * TQ
TK = 256
MOST_STEPS = 32
OFFSETS = (3, 2, 1, 0)
SUMS = HEAD_SIZE + 8
SCALING = HEAD_SIZE ** (-0.5)
LOG2_SCALING = SCALING * math.log2(math.e)
MASKED = -2e30
LOWEST = -1e30
F32 = jnp.float32
BF16 = jnp.bfloat16


def dot_nt(a, b):
    return lax.dot_general(a, b, (((1,), (1,)), ((), ())), preferred_element_type=F32)


def dot_nn(a, b):
    return lax.dot_general(a, b, (((1,), (0,)), ((), ())), preferred_element_type=F32)


def step_bias(lo_row, meta, n):
    start, first, last = meta[1, n], meta[2, n], meta[3, n]
    own = lax.broadcasted_iota(jnp.int32, (1, TQ), 1) + ((PAIRS - 1) * BLOCK + meta[0, n] * TQ)
    keys = lax.broadcasted_iota(jnp.int32, (TK, TQ), 0) + start
    seen = (keys >= jnp.maximum(lo_row, first)) & (keys <= jnp.minimum(own, last))
    return jnp.where(seen, 0.0, MASKED).astype(F32)


def list_steps(scalars, meta):
    count = jnp.int32(0)
    for tile in range(TILES):
        end = (PAIRS - 1) * BLOCK + (tile + 1) * TQ
        while end > 0:
            start = max(end - TK, 0)
            block = start // BLOCK
            border = (block + 1) * BLOCK
            first = jnp.where(scalars[TILES + PAIRS - 1 - block] == 1, start, border)
            last = jnp.int32(end - 1)
            if border < end:
                last = jnp.where(scalars[TILES + PAIRS - 2 - block] == 1, last, border - 1)
            meta[0, count] = tile
            meta[1, count] = start
            meta[2, count] = first
            meta[3, count] = last
            used = jnp.maximum(first, scalars[tile]) <= last
            count = count + used.astype(jnp.int32)
            end = end - TK
    for extra in range(2):
        meta[0, count + extra] = 0
        meta[1, count + extra] = 0
        meta[2, count + extra] = PAIRS * BLOCK
        meta[3, count + extra] = 0
    return count


def run_steps(count, stage1, stage2, buf_a, buf_b):
    stage1(0, buf_a)

    def body(j, carry):
        stage1(2 * j + 1, buf_b)
        stage2(2 * j, buf_a)
        stage1(2 * j + 2, buf_a)
        stage2(2 * j + 1, buf_b)
        return carry

    lax.fori_loop(0, (count + 1) // 2, body, 0)


def rows_of(start):
    return pl.ds(pl.multiple_of(start, TQ), TK)


def pack_kernel(q_ref, do_ref, x_ref, wide_s, x_s, in_sem, out_sem):
    width = HEADS_PER_GROUP * HEAD_SIZE
    wide = [
        [
            pltpu.make_async_copy(
                ref.at[:, pl.ds(group * width, width)], wide_s.at[i, group], in_sem.at[i, group]
            )
            for i, ref in enumerate((q_ref, do_ref))
        ]
        for group in range(TILES)
    ]
    for copy in sum(wide, []):
        copy.start()
    out_copies = []
    for group in range(TILES):
        for i in range(2):
            wide[group][i].wait()
            for h in range(HEADS_PER_GROUP):
                piece = wide_s[i, group, :, h * HEAD_SIZE : (h + 1) * HEAD_SIZE]
                x_s[group, i * HEADS_PER_GROUP + h] = piece
        out_copies.append(pltpu.make_async_copy(x_s.at[group], x_ref.at[group], out_sem.at[group]))
        out_copies[-1].start()
    for copy in out_copies:
        copy.wait()


def pack_kv_kernel(place, key_ref, value_ref, *outs):
    for d, out_ref in enumerate(outs):
        group = (place[0] + d) % TILES
        columns = pl.ds(pl.multiple_of(group * HEAD_SIZE, HEAD_SIZE), HEAD_SIZE)
        out_ref[0] = key_ref[:, columns]
        out_ref[1] = value_ref[:, columns]


def attend_kernel(heads, first_head, first_call, last_call, scalars, x_ref, *refs):
    kvs, lo_ref, refs = refs[0:PAIRS], refs[PAIRS], refs[PAIRS + 1 :]
    if not first_call:
        dk_in, dv_in, refs = refs[0], refs[1], refs[4:]
    att_ref, dq_ref, refs = refs[0], refs[1], refs[2:]
    if last_call:
        outs, refs = refs[0:PAIRS], refs[PAIRS:]
    else:
        dk_out, dv_out, refs = refs[0], refs[1], refs[2:]
    m_s, acc_s, dqt_s, dk_s, dv_s, delta_s, k_s, kt_s, v_s, vt_s = refs[:10]
    buf_a, buf_b, stash_s, top_s, att_s, meta, sem = refs[10:]
    lanes_all = heads * TQ
    if not last_call:
        dk_s, dv_s = dk_out, dv_out

    def queries(tile):
        return x_ref[tile, 0:heads].reshape(lanes_all, HEAD_SIZE)

    def cotangents(tile):
        return x_ref[tile, heads : 2 * heads].reshape(lanes_all, HEAD_SIZE)

    def columns(h):
        return slice(h * TQ, (h + 1) * TQ)

    def put(tile, ref, kind):
        return pltpu.make_async_copy(
            att_s.at[tile],
            ref.at[pl.ds(tile * TQ, TQ), pl.ds(first_head * TQ, lanes_all)],
            sem.at[kind, tile],
        )

    for slot, kv in enumerate(reversed(kvs)):
        for part in range(TILES):
            tokens = (scalars[2 * TILES] + TILES - part) % TILES
            place = pl.ds(pl.multiple_of(slot * BLOCK + tokens * TQ, TQ), TQ)
            key, value = kv[part, 0], kv[part, 1]
            k_s[place, :] = key
            kt_s[:, place] = key.T
            v_s[place, :] = value
            vt_s[0:HEAD_SIZE, place] = value.T
    vt_s[HEAD_SIZE:SUMS, :] = jnp.ones((SUMS - HEAD_SIZE, PAIRS * BLOCK), BF16)
    m_s[...] = jnp.full_like(m_s, LOWEST)
    acc_s[...] = jnp.zeros_like(acc_s)
    count = list_steps(scalars, meta)

    def scores(n, buf):
        buf[...] = dot_nt(k_s[rows_of(meta[1, n]), :], queries(meta[0, n]))

    def weigh(n, buf):
        tile = meta[0, n]
        bias = step_bias(lo_ref[tile], meta, n)
        val_t = vt_s[:, rows_of(meta[1, n])]
        m_old = m_s[tile]
        weights, tops = [], []
        for h in range(heads):
            s = buf[:, columns(h)] * LOG2_SCALING + bias
            top = jnp.maximum(m_old[:, columns(h)], jnp.max(s, axis=0, keepdims=True))
            weights.append(jnp.exp2(s - top).astype(BF16))
            tops.append(top)
        p = jnp.concatenate(weights, axis=1)
        m_new = jnp.concatenate(tops, axis=1)
        stash_s[n] = p
        top_s[n] = m_new
        m_s[tile] = m_new
        acc_s[tile] = acc_s[tile] * jnp.exp2(m_old - m_new) + dot_nn(val_t, p)

    run_steps(count, scores, weigh, buf_a, buf_b)
    ones = jnp.ones((8, 2 * HEAD_SIZE), BF16)
    for tile in range(TILES):
        total = acc_s[tile, HEAD_SIZE : HEAD_SIZE + 1, :]
        m_s[tile] = m_s[tile] + jnp.log2(total)
        inverse = 1.0 / total
        halves = []
        for h in range(heads):
            out = (acc_s[tile, 0:HEAD_SIZE, columns(h)] * inverse[:, columns(h)]).astype(BF16).T
            att_s[tile, :, columns(h)] = out
            product = out.astype(F32) * x_ref[tile, heads + h].astype(F32)
            high = product.astype(BF16)
            low = (product - high.astype(F32)).astype(BF16)
            halves.append(jnp.concatenate([high, low], axis=1))
        delta_s[tile] = dot_nt(ones, jnp.concatenate(halves, axis=0))[0:1]
        put(tile, att_ref, 0).start()
    if first_call:
        dk_s[...] = jnp.zeros_like(dk_s)
        dv_s[...] = jnp.zeros_like(dv_s)
    else:
        dk_s[...] = dk_in[...]
        dv_s[...] = dv_in[...]
    dqt_s[...] = jnp.zeros_like(dqt_s)

    def prob_grads(n, buf):
        buf[...] = dot_nt(v_s[rows_of(meta[1, n]), :], cotangents(meta[0, n]))

    def gradients(n, buf):
        tile, rows = meta[0, n], rows_of(meta[1, n])
        factor = jnp.exp2(top_s[n] - m_s[tile])
        delta = delta_s[tile]
        weights, grads = [], []
        for h in range(heads):
            p = stash_s[n, :, columns(h)].astype(F32) * factor[:, columns(h)]
            weights.append(p.astype(BF16))
            grads.append((p * (buf[:, columns(h)] - delta[:, columns(h)])).astype(BF16))
        p = jnp.concatenate(weights, axis=1)
        g = jnp.concatenate(grads, axis=1)
        dv_s[rows, :] += dot_nn(p, cotangents(tile))
        dk_s[rows, :] += dot_nn(g, queries(tile))
        dqt_s[tile] += dot_nn(kt_s[:, rows], g)

    run_steps(count, prob_grads, gradients, buf_a, buf_b)
    for tile in range(TILES):
        put(tile, att_ref, 0).wait()
        for h in range(heads):
            att_s[tile, :, columns(h)] = (dqt_s[tile, :, columns(h)] * SCALING).astype(BF16).T
        put(tile, dq_ref, 1).start()
    if last_call:
        for slot in range(PAIRS):
            kind = outs[slot].dtype
            for part in range(TILES):
                place = slice(slot * BLOCK + part * TQ, slot * BLOCK + (part + 1) * TQ)
                outs[slot][part, 0] = (dk_s[place, :] * SCALING).astype(kind)
                outs[slot][part, 1] = dv_s[place, :].astype(kind)
    for tile in range(TILES):
        put(tile, dq_ref, 1).wait()


def vmem():
    return pl.BlockSpec(memory_space=pltpu.VMEM)


def smem():
    return pl.BlockSpec(memory_space=pltpu.SMEM)


def pack(queries, cotangents):
    tokens = queries.shape[0]
    hbm = pl.BlockSpec(memory_space=pltpu.HBM)
    both = (TILES, 2 * HEADS_PER_GROUP, tokens, HEAD_SIZE)
    return pl.pallas_call(
        pack_kernel,
        in_specs=[hbm] * 2,
        out_specs=hbm,
        out_shape=jax.ShapeDtypeStruct(both, BF16),
        scratch_shapes=[
            pltpu.VMEM((2, TILES, tokens, HEADS_PER_GROUP * HEAD_SIZE), BF16),
            pltpu.VMEM(both, BF16),
            pltpu.SemaphoreType.DMA((2, TILES)),
            pltpu.SemaphoreType.DMA((TILES,)),
        ],
        compiler_params=pltpu.CompilerParams(vmem_limit_bytes=60 << 20),
        name="pack",
    )(queries, cotangents)


def pack_kv(place, keys, values):
    shape = jax.ShapeDtypeStruct((2, keys.shape[0], HEAD_SIZE), BF16)
    return pl.pallas_call(
        pack_kv_kernel,
        in_specs=[smem(), vmem(), vmem()],
        out_specs=[vmem()] * TILES,
        out_shape=[shape] * TILES,
        name="pack_kv",
    )(place, keys, values)


def attend(scalars, x, kvs, lo, first_head, carried):
    rows = PAIRS * BLOCK
    heads = x.shape[1] // 2
    lanes = heads * TQ
    first_call, last_call = not carried, first_head + heads == HEADS_PER_GROUP
    hbm = pl.BlockSpec(memory_space=pltpu.HBM)
    result = jax.ShapeDtypeStruct((BLOCK, LANES), BF16)
    sums = [jax.ShapeDtypeStruct((rows, HEAD_SIZE), F32)] * 2
    grad_shape = (TILES, 2, TQ, HEAD_SIZE)
    parts = [jax.ShapeDtypeStruct(grad_shape, F32 if o == 0 else BF16) for o in OFFSETS]
    more = parts if last_call else sums
    return pl.pallas_call(
        functools.partial(attend_kernel, heads, first_head, first_call, last_call),
        in_specs=[smem()] + [vmem()] * (PAIRS + 2) + [vmem(), vmem(), hbm, hbm][: len(carried)],
        out_specs=[hbm, hbm] + [vmem()] * len(more),
        out_shape=[result, result] + more,
        input_output_aliases={} if first_call else {PAIRS + 5: 0, PAIRS + 6: 1},
        scratch_shapes=[
            pltpu.VMEM((TILES, 1, lanes), F32),
            pltpu.VMEM((TILES, SUMS, lanes), F32),
            pltpu.VMEM((TILES, HEAD_SIZE, lanes), F32),
            pltpu.VMEM((rows if last_call else 8, HEAD_SIZE), F32),
            pltpu.VMEM((rows if last_call else 8, HEAD_SIZE), F32),
            pltpu.VMEM((TILES, 1, lanes), F32),
            pltpu.VMEM((rows, HEAD_SIZE), BF16),
            pltpu.VMEM((HEAD_SIZE, rows), BF16),
            pltpu.VMEM((rows, HEAD_SIZE), BF16),
            pltpu.VMEM((SUMS, rows), BF16),
            pltpu.VMEM((TK, lanes), F32),
            pltpu.VMEM((TK, lanes), F32),
            pltpu.VMEM((MOST_STEPS, TK, lanes), BF16),
            pltpu.VMEM((MOST_STEPS, 1, lanes), F32),
            pltpu.VMEM((TILES, TQ, lanes), BF16),
            pltpu.SMEM((4, MOST_STEPS), jnp.int32),
            pltpu.SemaphoreType.DMA((2, TILES)),
        ],
        compiler_params=pltpu.CompilerParams(vmem_limit_bytes=(12 + 3 * heads) << 20),
        cost_estimate=pl.CostEstimate(
            flops=2 * 6 * heads * 512 * 1280 * 128 * 2, bytes_accessed=8 << 20, transcendentals=0
        ),
        name="attend_%d" % first_head,
    )(scalars, x, *kvs, lo, *carried)


def passed_along(value, axis, steps):
    count = lax.axis_size(axis)
    initial, last = (max(0, -steps), min(count, count - steps))
    return lax.ppermute(value, axis, [(source, source + steps) for source in range(initial, last)])


def exchange(value):
    return lax.all_to_all(value, "tp", split_axis=0, concat_axis=0, tiled=True)


def window_start(doc_ids, blk):
    begin = jnp.maximum(blk - (PAIRS - 1), 0) * BLOCK
    window = lax.dynamic_slice_in_dim(doc_ids, begin, PAIRS * BLOCK)
    own = lax.dynamic_slice_in_dim(doc_ids, blk * BLOCK, BLOCK)
    before = jnp.sum((window[:, None] < own[None, :]).astype(jnp.int32), axis=0)
    return before + begin - (blk - (PAIRS - 1)) * BLOCK


def bounds(lo, live, place):
    return lo.reshape(TILES, 1, TQ), jnp.concatenate([lo[::TQ], live, place])


def local(queries, key_states, value_projection, output_gradient, doc_ids, pair_live):
    blk = lax.axis_index("ctx")
    place = lax.axis_index("tp").astype(jnp.int32).reshape(1)
    own, *pieces = pack_kv(place, key_states, value_projection)
    for d, piece in enumerate(pieces, start=1):
        pieces[d - 1] = lax.ppermute(piece, "tp", [(i, (i + d) % TILES) for i in range(TILES)])
    queries, output_gradient, own = lax.optimization_barrier((queries, output_gradient, own))
    x = pack(queries, output_gradient)
    x, own, *pieces = lax.optimization_barrier((x, own, *pieces))
    x = exchange(x)
    kv0 = jnp.stack([own] + pieces)
    lo, scalars = bounds(window_start(doc_ids, blk), pair_live[0], place)
    kv2 = passed_along(kv0, "ctx", 2)
    kv1 = passed_along(kv0, "ctx", 1)
    kv3 = passed_along(kv2, "ctx", 1)
    kvs = [kv0, kv1, kv2, kv3]
    attention, dq, part3, part2, part1, part0 = attend(scalars, x, kvs, lo, 0, ())
    got3 = passed_along(part3, "ctx", -1)
    got1 = passed_along(part1, "ctx", -1)
    part2 = (part2.astype(F32) + got3.astype(F32)).astype(BF16)
    got2 = passed_along(part2, "ctx", -2)
    total = part0 + got1.astype(F32) + got2.astype(F32)
    key_grad = total[:, 0].reshape(BLOCK, HEAD_SIZE).astype(BF16)
    value_grad = total[:, 1].reshape(BLOCK, HEAD_SIZE).astype(BF16)
    return (attention, dq, key_grad, value_grad)


def solution(mesh):
    in_specs = (
        P(("ctx", "tp"), None),
        P(("ctx", "tp"), None),
        P(("ctx", "tp"), None),
        P(("ctx", "tp"), None),
        P(),
        P("ctx", None),
    )
    out_specs = (P("ctx", "tp"), P("ctx", "tp"), P("ctx", "tp"), P("ctx", "tp"))
    return jax.shard_map(local, mesh=mesh, in_specs=in_specs, out_specs=out_specs, check_vma=False)
```
